256 devices in a mesh: feat: 128 (over z, y, x), rel: 2 (over core).
Axes of the slice: x: 4, y: 4, z: 8, core: 2. Of those that a mesh axis runs over, the one named last changes fastest.
Arguments:
- features: bfloat16 [768, 16384], P(None, 'feat'), may hold values from -6 to 6
- rel_weight: bfloat16 [4, 768, 768], P('rel'), may hold values from -0.21875 to 0.21875
- self_weight: bfloat16 [768, 768], P('rel'), may hold values from -0.21875 to 0.21875
- block_rows: int32 [4, 64], P('rel'), may hold values from 0 to 127
- block_cols: int32 [4, 64], P('rel'), may hold values from 0 to 127, as said below
- count_tiles: int32 [4, 64, 128, 128], P('rel'), may hold values from 0 to 3
- live_slots: int32 [4], P('rel'), may hold values from 32 to 64, as said below
- degrees: int32 [4, 16384], P('rel', 'feat'), may hold values from 16 to 127
Outputs:
- mixed: bfloat16 [768, 16384], P(None, 'feat')
The draws below stay inside these ranges and needn't reach their ends.
Inputs may be any that keep to these rules, and one draw needn't show every extreme that they name: Slots at or beyond live_slots[r] are unused; at least 32 slots of each relation are used, one relation uses all 64 and one exactly 32. `block_cols`: over the first 32 slots of all relations together every source block occurs.
All inputs are finite; a program needn't handle non-finite values.
Results may differ from the reference program's by a relative error of at most 0.0034.
Values may be sent and summed in bfloat16 or wider, within the bound.
No kernel may reach another device: no remote copies, remote signals or barrier semaphores. Data moves between devices by JAX's collectives and lax.ppermute only.
A program may use at most 64 MiB of HBM per device.

```python
import math
import jax
import jax.numpy as jnp
import numpy as np
from jax import lax

D = 768
BLOCK = 128
NNZB = 64
RELS = 4
NODES = 16384
BLOCKS = 128


def draw_block_cols(key, part):
    key = jax.random.fold_in(key, 11)
    key_perm, key_rest = jax.random.split(key)
    order = jax.random.permutation(key_perm, BLOCKS)
    slot_ids = jnp.arange(NNZB)
    cover_ids = (jnp.arange(RELS)[:, None] * (NNZB // 2) + slot_ids[None, :]) % BLOCKS
    covered = order[cover_ids]
    scattered = jax.random.randint(key_rest, (RELS, NNZB), 0, BLOCKS)
    return jnp.where(slot_ids[None, :] < NNZB // 2, covered, scattered).astype(jnp.int32)


def draw_live_slots(key, part):
    key = jax.random.fold_in(key, 23)
    key_base, key_order = jax.random.split(key)
    base_counts = jax.random.randint(key_base, (RELS,), NNZB // 2, NNZB + 1)
    order = jax.random.permutation(key_order, RELS)
    base_counts = base_counts.at[order[0]].set(NNZB).at[order[1]].set(NNZB // 2)
    return base_counts.astype(jnp.int32)


def set_ends(drawn, stream_key, low, largest):
    longest = drawn.shape.index(max(drawn.shape))
    spots = []
    for shift in (0, 1):
        where = [jax.random.randint(jax.random.fold_in(stream_key, axis), (), 0, length) for axis, length in enumerate(drawn.shape)]
        where[longest] = (where[longest] + shift) % drawn.shape[longest]
        spots.append(tuple(where))
    return drawn.at[spots[0]].set(low).at[spots[1]].set(largest)


def shard_levels(own_key, shape, cuts, low, high):
    loudness, own = 1.0, jax.random.fold_in(own_key, 6)
    for dim, blocks in cuts:
        draws = jnp.exp(jax.random.uniform(jax.random.fold_in(own, dim), (blocks,), jnp.float32, low / len(cuts), high / len(cuts)))
        loudness = loudness * jnp.repeat(draws, shape[dim] // blocks).reshape([-1 if axis == dim else 1 for axis in range(len(shape))])
    return loudness


def rank_bounds(number_of, slope):
    portions = [(1 << 20) // math.isqrt(standing ** slope) + 1 for standing in range(1, number_of + 1)]
    deviation = 1 + sum(portions) // (1 << 30)
    return np.cumsum(np.array([max(1, weight // deviation) for weight in portions]))


def ranked_ids(own_key, extent, number_of, skew):
    grid = rank_bounds(number_of, skew)
    ticket = jax.random.randint(jax.random.fold_in(own_key, 1), extent, 0, int(grid[number_of - 1]))
    standing = jnp.searchsorted(jnp.asarray(grid, jnp.int32), ticket, side="right")
    return jax.random.permutation(jax.random.fold_in(own_key, 2), number_of)[standing].astype(jnp.int32)


def noise(stream_key, shape, width, reach, shards=(), kind=jnp.bfloat16):
    array = width * jax.random.normal(stream_key, shape, jnp.float32)
    if shards:
        array = array * shard_levels(stream_key, shape, shards, -0.22, 0.18)
    return jnp.clip(array, -reach, reach).astype(kind)


def setup_inputs(seed: int = 0) -> dict:
    keys = jax.random.split(jax.random.key(seed), 9)
    features = noise(keys[0], (D, NODES), 1.0, 6.0, ((1, 128),))
    rel_weight = noise(keys[1], (RELS, D, D), D ** -0.5, 0.21875, ((0, 2),))
    self_weight = noise(keys[2], (D, D), D ** -0.5, 0.21875, ((0, 2),))
    block_rows = set_ends(ranked_ids(keys[3], (RELS, NNZB), BLOCKS, 2), jax.random.fold_in(keys[3], 3), 0, BLOCKS - 1).astype(jnp.int32)
    block_cols = draw_block_cols(jax.random.fold_in(keys[8], 71), 0)
    count_tiles = set_ends(jax.random.randint(keys[5], (RELS, NNZB, BLOCK, BLOCK), 0, 4), jax.random.fold_in(keys[5], 1), 0, 3).astype(jnp.int32)
    live_slots = draw_live_slots(jax.random.fold_in(keys[8], 71), 0)
    degrees = set_ends(jax.random.randint(keys[7], (RELS, NODES), 16, 128), jax.random.fold_in(keys[7], 1), 16, 127).astype(jnp.int32)
    return {"features": features, "rel_weight": rel_weight, "self_weight": self_weight, "block_rows": block_rows, "block_cols": block_cols, "count_tiles": count_tiles, "live_slots": live_slots, "degrees": degrees}


def relation_sum(features, rows_r, cols_r, tiles_r, count_r):
    block_size = tiles_r.shape[1]

    def one_slot(slot_index, accumulated):
        row_start = (rows_r[slot_index] * block_size).astype(jnp.int32)
        col_start = (cols_r[slot_index] * block_size).astype(jnp.int32)
        panel = lax.dynamic_slice_in_dim(features, col_start, block_size, 1)
        tile_now = tiles_r[slot_index].astype(jnp.bfloat16)
        contrib = lax.dot_general(panel, tile_now, (((1,), (1,)), ((), ())), preferred_element_type=jnp.float32)
        current = lax.dynamic_slice_in_dim(accumulated, row_start, block_size, 1)
        return lax.dynamic_update_slice_in_dim(accumulated, current + contrib, row_start, 1)

    return lax.fori_loop(0, count_r, one_slot, jnp.zeros(features.shape, jnp.float32))


def reference(features, rel_weight, self_weight, block_rows, block_cols, count_tiles, live_slots, degrees):
    dims = (((0,), (0,)), ((), ()))
    total_sum = lax.dot_general(self_weight, features, dims, preferred_element_type=jnp.float32)
    for relation in range(RELS):
        summed = relation_sum(features, block_rows[relation], block_cols[relation], count_tiles[relation], live_slots[relation])
        hidden = (summed / degrees[relation].astype(jnp.float32)[None, :]).astype(jnp.bfloat16)
        total_sum = total_sum + lax.dot_general(rel_weight[relation], hidden, dims, preferred_element_type=jnp.float32)
    return jnp.maximum(total_sum, 0.0).astype(jnp.bfloat16)
```

```python
import functools

import jax
import jax.numpy as jnp
from jax import lax
from jax.experimental import pallas as pl
from jax.experimental.pallas import tpu as pltpu
from jax.sharding import PartitionSpec as P

GROUP = 8


def spread_matrix(out_rows, in_rows, stride, take):
    out_id = lax.broadcasted_iota(jnp.int32, (out_rows, in_rows), 0)
    in_id = lax.broadcasted_iota(jnp.int32, (out_rows, in_rows), 1)
    place = out_id // stride * take + out_id % stride
    return jnp.where((out_id % stride < take) & (place == in_id), 1.0, 0.0).astype(jnp.bfloat16)


def pack_kernel(features_ref, degrees_ref, out_ref):
    take = features_ref.shape[0] // out_ref.shape[0]
    width = features_ref.shape[1]
    spread = spread_matrix(128, 16 * take, 8, take)
    degrees = degrees_ref[...].astype(jnp.float32)
    row = lax.broadcasted_iota(jnp.int32, (8, width), 0)
    tail = jnp.where(row == take, degrees[0:1], jnp.where(row == take + 1, degrees[1:2], 0.0))
    for block in range(out_ref.shape[0] // 16):
        rows = features_ref[block * 16 * take : (block + 1) * 16 * take, :]
        placed = jnp.dot(spread, rows, preferred_element_type=jnp.float32)
        out_ref[block * 16 : (block + 1) * 16] = (placed.reshape(16, 8, width) + tail[None]).astype(
            jnp.bfloat16
        )


def slots_kernel(rows_ref, cols_ref, live_ref, panels_ref, tiles_ref, out_ref, sums_ref):
    sums_ref[...] = jnp.zeros_like(sums_ref)
    relations, blocks = sums_ref.shape[0], sums_ref.shape[1]
    for relation in range(relations):
        live = live_ref[relation]

        def group(index, carry, relation=relation, live=live):
            base = index * GROUP
            parts = []
            for step in range(GROUP):
                slot = base + step
                panel = panels_ref[cols_ref[relation, slot]]
                tile = tiles_ref[relation, slot].astype(jnp.float32).astype(jnp.bfloat16)
                part = lax.dot_general(
                    panel, tile, (((1,), (1,)), ((), ())), preferred_element_type=jnp.float32
                )
                parts.append(jnp.where(slot < live, part, 0.0))
            for step in range(GROUP):
                row = rows_ref[relation, base + step]
                sums_ref[relation, row] += parts[step]
            return carry

        lax.fori_loop(0, pl.cdiv(live, GROUP), group, 0)

    def finish(index, carry):
        at = pl.ds(index * 8, 8)
        packed = panels_ref[at].astype(jnp.float32)
        take = 8 - relations
        done = [
            sums_ref[relation, at] / packed[:, take + relation : take + relation + 1, :]
            for relation in range(relations)
        ]
        out_ref[at] = jnp.concatenate(done, axis=1).astype(jnp.bfloat16)
        return carry

    lax.fori_loop(0, blocks // 8, finish, 0)


def weights_kernel(rel_ref, self_ref, features_ref, packed_ref, own_ref):
    take = rel_ref.shape[1] // 128
    relations = rel_ref.shape[0]
    rows = 16 * take
    width = 16 * 8 * relations
    out_id = lax.broadcasted_iota(jnp.int32, (rows * relations, width), 1)
    in_id = lax.broadcasted_iota(jnp.int32, (rows * relations, width), 0)
    inner = out_id % 8
    place = (out_id // 8 % relations) * rows + out_id // (8 * relations) * take + inner
    pick = jnp.where((inner < take) & (place == in_id), 1.0, 0.0).astype(jnp.bfloat16)
    for block in range(8):
        part = jnp.concatenate(
            [rel_ref[relation, block * rows : (block + 1) * rows, :] for relation in range(relations)], axis=0
        )
        packed_ref[:, block * width : (block + 1) * width] = lax.dot_general(
            part, pick, (((0,), (0,)), ((), ())), preferred_element_type=jnp.float32
        ).astype(jnp.bfloat16)
    half = self_ref.shape[0]
    start = pl.multiple_of(lax.axis_index("rel") * half, half)
    own_ref[...] = lax.dot_general(
        self_ref[...],
        features_ref[pl.ds(start, half), :],
        (((0,), (0,)), ((), ())),
        preferred_element_type=jnp.float32,
    )


def transform_kernel(packed_ref, hidden_ref, own_ref, out_ref):
    hidden = hidden_ref[...].reshape(packed_ref.shape[1], hidden_ref.shape[2])
    out_ref[...] = own_ref[...] + jnp.dot(packed_ref[...], hidden, preferred_element_type=jnp.float32)


VMEM = pl.BlockSpec(memory_space=pltpu.VMEM)
SMEM = pl.BlockSpec(memory_space=pltpu.SMEM)


def shards(
    features, rel_weight, self_weight, block_rows, block_cols, count_tiles, live_slots, degrees
):
    width_all, node_local = features.shape
    relations = rel_weight.shape[0]
    devices = 128
    send = pl.pallas_call(
        pack_kernel,
        out_shape=jax.ShapeDtypeStruct((devices, 8, node_local), jnp.bfloat16),
        in_specs=[VMEM, VMEM],
        out_specs=VMEM,
        name="pack",
    )(features, degrees)
    panels = lax.all_to_all(send, "feat", split_axis=0, concat_axis=0, tiled=True)
    packed_weight, own = pl.pallas_call(
        weights_kernel,
        out_shape=(
            jax.ShapeDtypeStruct((width_all, devices * 8 * relations), jnp.bfloat16),
            jax.ShapeDtypeStruct((width_all, node_local), jnp.float32),
        ),
        in_specs=[VMEM, VMEM, VMEM],
        out_specs=(VMEM, VMEM),
        compiler_params=pltpu.CompilerParams(vmem_limit_bytes=24 * 1024 * 1024),
        name="weights",
    )(rel_weight, self_weight, features)
    hidden = pl.pallas_call(
        slots_kernel,
        out_shape=jax.ShapeDtypeStruct((devices, 8 * relations, node_local), jnp.bfloat16),
        in_specs=[SMEM, SMEM, SMEM, VMEM, VMEM],
        out_specs=VMEM,
        scratch_shapes=[pltpu.VMEM((relations, devices, 8, node_local), jnp.float32)],
        compiler_params=pltpu.CompilerParams(vmem_limit_bytes=32 * 1024 * 1024),
        name="slots",
    )(block_rows, block_cols, live_slots, panels, count_tiles)
    gathered = lax.all_to_all(hidden, "feat", split_axis=0, concat_axis=0, tiled=True)
    partial_sum = pl.pallas_call(
        transform_kernel,
        out_shape=jax.ShapeDtypeStruct((width_all, node_local), jnp.float32),
        in_specs=[VMEM, VMEM, VMEM],
        out_specs=VMEM,
        compiler_params=pltpu.CompilerParams(vmem_limit_bytes=24 * 1024 * 1024),
        name="transform",
    )(packed_weight, gathered, own)
    other = lax.ppermute(partial_sum, "rel", [(0, 1), (1, 0)])
    return jnp.maximum(partial_sum + other, 0.0).astype(jnp.bfloat16)


def solution(mesh):
    placed = (
        P(None, "feat"),
        P("rel", None, None),
        P("rel", None),
        P("rel", None),
        P("rel", None),
        P("rel", None, None, None),
        P("rel"),
        P("rel", "feat"),
    )
    return jax.shard_map(
        shards, mesh=mesh, in_specs=placed, out_specs=P(None, "feat"), check_vma=False
    )
```

```python
import functools

import jax
import jax.numpy as jnp
from jax import lax
from jax.experimental import pallas as pl
from jax.experimental.pallas import tpu as pltpu
from jax.sharding import PartitionSpec as P

GROUP = 32
CHUNK = 8
MIB = 1024 * 1024


def spread_matrix(out_rows, in_rows, stride, take):
    out_id = lax.broadcasted_iota(jnp.int32, (out_rows, in_rows), 0)
    in_id = lax.broadcasted_iota(jnp.int32, (out_rows, in_rows), 1)
    place = out_id // stride * take + out_id % stride
    return jnp.where((out_id % stride < take) & (place == in_id), 1.0, 0.0).astype(jnp.bfloat16)


def pack_kernel(features_ref, degrees_ref, out_ref):
    take = features_ref.shape[0] // out_ref.shape[0]
    width = features_ref.shape[1]
    spread = spread_matrix(128, 16 * take, 8, take)
    degrees = degrees_ref[...].astype(jnp.float32)
    row = lax.broadcasted_iota(jnp.int32, (8, width), 0)
    tail = jnp.where(row == take, degrees[0:1], jnp.where(row == take + 1, degrees[1:2], 0.0))
    for block in range(out_ref.shape[0] // 16):
        rows = features_ref[block * 16 * take : (block + 1) * 16 * take, :]
        placed = jnp.dot(spread, rows, preferred_element_type=jnp.float32)
        out_ref[block * 16 : (block + 1) * 16] = (placed.reshape(16, 8, width) + tail[None]).astype(
            jnp.bfloat16
        )


def tiles_kernel(tiles_ref, after_ref, out_ref, landing_ref, arrived_ref):
    del after_ref
    chunks, per_chunk = landing_ref.shape[0], landing_ref.shape[1]
    per_relation = tiles_ref.shape[1] // per_chunk

    def fetch(chunk):
        source = tiles_ref.at[chunk // per_relation, pl.ds(chunk % per_relation * per_chunk, per_chunk)]
        return pltpu.make_async_copy(source, landing_ref.at[chunk], arrived_ref.at[chunk])

    for chunk in range(chunks):
        fetch(chunk).start()

    def turn(chunk, carry):
        fetch(chunk).wait()
        for pair in range(per_chunk // 2):
            turned = [landing_ref[chunk, 2 * pair + side].astype(jnp.float32).T for side in range(2)]
            counts = jnp.concatenate(turned, axis=1).astype(jnp.int32).astype(jnp.int8)
            out_ref[chunk * (per_chunk // 2) + pair] = counts
        return carry

    lax.fori_loop(0, chunks, turn, 0)


def slots_kernel(rows_ref, cols_ref, live_ref, panels_ref, tiles_ref, out_ref, sums_ref):
    sums_ref[...] = jnp.zeros_like(sums_ref)
    relations, blocks, _, width = sums_ref.shape
    pairs = tiles_ref.shape[0] // relations
    for relation in range(relations):
        live = live_ref[relation]

        def group(index, carry, relation=relation, live=live):
            base = index * GROUP
            parts = []
            for step in range(0, GROUP, 2):
                slot = base + step
                panel = jnp.concatenate(
                    [panels_ref[cols_ref[relation, slot + side]] for side in range(2)], axis=0
                )
                tile = tiles_ref[relation * pairs + index * (GROUP // 2) + step // 2].astype(jnp.bfloat16)
                both = jnp.dot(panel, tile, preferred_element_type=jnp.float32)
                parts += [both[:8, :width], both[8:, width:]]
            for step in range(GROUP):
                slot = base + step
                sums_ref[relation, rows_ref[relation, slot]] += jnp.where(slot < live, parts[step], 0.0)
            return carry

        lax.fori_loop(0, pl.cdiv(live, GROUP), group, 0)

    def finish(index, carry):
        at = pl.ds(index * 8, 8)
        packed = panels_ref[at].astype(jnp.float32)
        take = 8 - relations
        done = [
            sums_ref[relation, at] / packed[:, take + relation : take + relation + 1, :]
            for relation in range(relations)
        ]
        out_ref[at] = jnp.concatenate(done, axis=1).astype(jnp.bfloat16)
        return carry

    lax.fori_loop(0, blocks // 8, finish, 0)


def weights_kernel(rel_ref, self_ref, features_ref, after_ref, turned_ref, own_ref):
    del after_ref
    depth = rel_ref.shape[1]
    for relation in range(rel_ref.shape[0]):
        for start in range(0, depth, 128):
            turned_ref[:, relation * depth + start : relation * depth + start + 128] = rel_ref[
                relation, start : start + 128, :
            ].T
    half = self_ref.shape[0]
    start = pl.multiple_of(lax.axis_index("rel") * half, half)
    own_ref[...] = lax.dot_general(
        self_ref[...],
        features_ref[pl.ds(start, half), :],
        (((0,), (0,)), ((), ())),
        preferred_element_type=jnp.float32,
    )


def transform_kernel(turned_ref, hidden_ref, own_ref, out_ref, sorted_ref):
    blocks, height, width = hidden_ref.shape
    relations = height // 8
    depth = sorted_ref.shape[0] // relations
    take = depth // blocks
    gather = 16 * take
    out_id = lax.broadcasted_iota(jnp.int32, (relations * gather, 16 * height), 0)
    in_id = lax.broadcasted_iota(jnp.int32, (relations * gather, 16 * height), 1)
    inner = out_id % gather
    place = inner // take * height + out_id // gather * 8 + inner % take
    pick = jnp.where(place == in_id, 1.0, 0.0).astype(jnp.bfloat16)
    for block in range(blocks // 16):
        rows = hidden_ref[block * 16 : (block + 1) * 16].reshape(16 * height, width)
        ordered = jnp.dot(pick, rows, preferred_element_type=jnp.float32).astype(jnp.bfloat16)
        for relation in range(relations):
            start = relation * depth + block * gather
            sorted_ref[start : start + gather, :] = ordered[relation * gather : (relation + 1) * gather]
    out_ref[...] = own_ref[...] + jnp.dot(
        turned_ref[...], sorted_ref[...], preferred_element_type=jnp.float32
    )


VMEM = pl.BlockSpec(memory_space=pltpu.VMEM)
SMEM = pl.BlockSpec(memory_space=pltpu.SMEM)
HBM = pl.BlockSpec(memory_space=pltpu.HBM)


def shards(
    features, rel_weight, self_weight, block_rows, block_cols, count_tiles, live_slots, degrees
):
    width_all, node_local = features.shape
    relations, slots, block_size, _ = count_tiles.shape
    devices = lax.axis_size("feat")
    send = pl.pallas_call(
        pack_kernel,
        out_shape=jax.ShapeDtypeStruct((devices, 8, node_local), jnp.bfloat16),
        in_specs=[VMEM, VMEM],
        out_specs=VMEM,
        compiler_params=pltpu.CompilerParams(vmem_limit_bytes=62 * MIB),
        name="pack",
    )(features, degrees)
    panels = lax.all_to_all(send, "feat", split_axis=0, concat_axis=0, tiled=True)
    chunks = relations * slots // CHUNK
    tiles = pl.pallas_call(
        tiles_kernel,
        out_shape=jax.ShapeDtypeStruct((relations * slots // 2, block_size, 2 * block_size), jnp.int8),
        in_specs=[HBM, HBM],
        out_specs=VMEM,
        scratch_shapes=[
            pltpu.VMEM((chunks, CHUNK, block_size, block_size), jnp.int32),
            pltpu.SemaphoreType.DMA((chunks,)),
        ],
        compiler_params=pltpu.CompilerParams(vmem_limit_bytes=50 * MIB),
        cost_estimate=pl.CostEstimate(flops=0, bytes_accessed=13 * MIB, transcendentals=0),
        name="tiles",
    )(count_tiles, send)
    hidden = pl.pallas_call(
        slots_kernel,
        out_shape=jax.ShapeDtypeStruct((devices, 8 * relations, node_local), jnp.bfloat16),
        in_specs=[SMEM, SMEM, SMEM, VMEM, VMEM],
        out_specs=VMEM,
        scratch_shapes=[pltpu.VMEM((relations, devices, 8, node_local), jnp.float32)],
        compiler_params=pltpu.CompilerParams(vmem_limit_bytes=8 * MIB),
        name="slots",
    )(block_rows, block_cols, live_slots, panels, tiles)
    gathered = lax.all_to_all(hidden, "feat", split_axis=0, concat_axis=0, tiled=True)
    turned_weight, own = pl.pallas_call(
        weights_kernel,
        out_shape=(
            jax.ShapeDtypeStruct((width_all, relations * width_all), jnp.bfloat16),
            jax.ShapeDtypeStruct((width_all, node_local), jnp.float32),
        ),
        in_specs=[VMEM, VMEM, VMEM, HBM],
        out_specs=(VMEM, VMEM),
        compiler_params=pltpu.CompilerParams(vmem_limit_bytes=12 * MIB),
        cost_estimate=pl.CostEstimate(flops=800_000_000, bytes_accessed=7 * MIB, transcendentals=0),
        name="weights",
    )(rel_weight, self_weight, features, hidden)
    partial_sum = pl.pallas_call(
        transform_kernel,
        out_shape=jax.ShapeDtypeStruct((width_all, node_local), jnp.float32),
        in_specs=[VMEM, VMEM, VMEM],
        out_specs=VMEM,
        scratch_shapes=[pltpu.VMEM((relations * width_all, node_local), jnp.bfloat16)],
        compiler_params=pltpu.CompilerParams(vmem_limit_bytes=8 * MIB),
        name="transform",
    )(turned_weight, gathered, own)
    other = lax.ppermute(partial_sum, "rel", [(0, 1), (1, 0)])
    return jnp.maximum(partial_sum + other, 0.0).astype(jnp.bfloat16)


def solution(mesh):
    placed = (
        P(None, "feat"),
        P("rel", None, None),
        P("rel", None),
        P("rel", None),
        P("rel", None),
        P("rel", None, None, None),
        P("rel"),
        P("rel", "feat"),
    )
    return jax.shard_map(
        shards, mesh=mesh, in_specs=placed, out_specs=P(None, "feat"), check_vma=False
    )
```

```python
import functools

import jax
import jax.numpy as jnp
from jax import lax
from jax.experimental import pallas as pl
from jax.experimental.pallas import tpu as pltpu
from jax.sharding import PartitionSpec as P

GROUP = 32
CHUNK = 8
PARTS = 1
FIRST = 74
MIB = 1024 * 1024


def pack_kernel(features_ref, degrees_ref, out_ref):
    blocks, height, width = out_ref.shape
    take = features_ref.shape[0] // blocks
    out_id = lax.broadcasted_iota(jnp.int32, (16 * height, 16 * take), 0)
    in_id = lax.broadcasted_iota(jnp.int32, (16 * height, 16 * take), 1)
    inner = out_id % height
    place = out_id // height * take + inner
    spread = jnp.where((inner < take) & (place == in_id), 1.0, 0.0).astype(jnp.bfloat16)
    row = lax.broadcasted_iota(jnp.int32, (height, width), 0)
    degrees = degrees_ref[...].astype(jnp.float32)
    tail = jnp.where(row == take, degrees[0:1], jnp.where(row == take + 1, degrees[1:2], 0.0))
    for start in range(0, blocks, 16):
        rows = features_ref[start * take : (start + 16) * take, :]
        placed = jnp.dot(spread, rows, preferred_element_type=jnp.float32).reshape(16, height, width)
        out_ref[start : start + 16] = (placed + tail[None]).astype(jnp.bfloat16)


def tiles_kernel(tiles_ref, self_ref, features_ref, out_ref, own_ref, landing_ref, arrived_ref):
    chunks, per_chunk = landing_ref.shape[0], landing_ref.shape[1]
    per_relation = tiles_ref.shape[1] // per_chunk

    def fetch(chunk):
        source = tiles_ref.at[chunk // per_relation, pl.ds(chunk % per_relation * per_chunk, per_chunk)]
        return pltpu.make_async_copy(source, landing_ref.at[chunk], arrived_ref.at[chunk])

    for chunk in range(chunks):
        fetch(chunk).start()
    half = self_ref.shape[0]
    start = pl.multiple_of(lax.axis_index("rel") * half, half)
    own_ref[...] = lax.dot_general(
        self_ref[...],
        features_ref[pl.ds(start, half), :],
        (((0,), (0,)), ((), ())),
        preferred_element_type=jnp.float32,
    )

    def turn(chunk, carry):
        fetch(chunk).wait()
        for pair in range(per_chunk // 2):
            turned = [landing_ref[chunk, 2 * pair + side].astype(jnp.float32).T for side in range(2)]
            counts = jnp.concatenate(turned, axis=1).astype(jnp.int32).astype(jnp.int8)
            out_ref[chunk * (per_chunk // 2) + pair] = counts
        return carry

    lax.fori_loop(0, chunks, turn, 0)


def slots_kernel(
    rows_hbm, cols_hbm, live_hbm, panels_ref, tiles_ref, out_ref, token_ref,
    rows_ref, cols_ref, live_ref, sums_ref, done_ref, in_sem, out_sem,
):
    pulls = [
        pltpu.make_async_copy(source, target, in_sem.at[index])
        for index, (source, target) in enumerate(
            ((rows_hbm, rows_ref), (cols_hbm, cols_ref), (live_hbm, live_ref))
        )
    ]
    for pull in pulls:
        pull.start()
    token_ref[...] = jnp.zeros_like(token_ref)
    sums_ref[...] = jnp.zeros_like(sums_ref)
    for pull in pulls:
        pull.wait()
    relations, blocks, height, width = sums_ref.shape
    take = height - relations
    pairs = tiles_ref.shape[0] // relations

    def position(block):
        return jnp.bitwise_xor(block, FIRST)

    def add_group(relation, base, live):
        parts = []
        for step in range(0, GROUP, 2):
            slot = base + step
            panel = jnp.concatenate(
                [panels_ref[position(cols_ref[relation, slot + side])] for side in range(2)], axis=0
            )
            tile = tiles_ref[relation * pairs + slot // 2].astype(jnp.bfloat16)
            both = jnp.dot(panel, tile, preferred_element_type=jnp.float32)
            parts += [both[:height, :width], both[height:, width:]]
        for step in range(GROUP):
            slot = base + step
            part = parts[step] if live is None else jnp.where(slot < live, parts[step], 0.0)
            sums_ref[relation, position(rows_ref[relation, slot])] += part

    for relation in range(relations):
        add_group(relation, 0, None)
    for relation in range(relations):
        live = live_ref[relation]
        for base in range(GROUP, rows_ref.shape[1], GROUP):
            pl.when(live > base)(functools.partial(add_group, relation, base, live))

    part_blocks = blocks // PARTS

    def store(part):
        at = pl.ds(part * part_blocks, part_blocks)
        return pltpu.make_async_copy(done_ref.at[at], out_ref.at[at], out_sem.at[part])

    for part in range(PARTS):

        def finish(index, carry, part=part):
            at = pl.ds(part * part_blocks + index * 8, 8)
            packed = panels_ref[at].astype(jnp.float32)
            first, second = [
                sums_ref[relation, at] / packed[:, take + relation : take + relation + 1, :]
                for relation in range(2)
            ]
            rest = jnp.concatenate([first[:, 4:6], second[:, 4:6]], axis=1)
            done_ref[at, :, 0:width] = first[:, 0:4].astype(jnp.bfloat16)
            done_ref[at, :, width : 2 * width] = second[:, 0:4].astype(jnp.bfloat16)
            done_ref[at, :, 2 * width : 3 * width] = rest.astype(jnp.bfloat16)
            return carry

        lax.fori_loop(0, part_blocks // 8, finish, 0)
        store(part).start()
    for part in range(PARTS):
        store(part).wait()


def weights_kernel(rel_ref, token_ref, turned_ref):
    del token_ref
    depth = rel_ref.shape[1]
    for relation in range(rel_ref.shape[0]):
        for start in range(0, depth, 128):
            turned_ref[:, relation * depth + start : relation * depth + start + 128] = rel_ref[
                relation, start : start + 128, :
            ].T


def transform_kernel(turned_ref, hidden_ref, own_ref, out_ref, sorted_ref):
    blocks = hidden_ref.shape[0]
    width = sorted_ref.shape[1]
    depth = sorted_ref.shape[0] // 2
    take = depth // blocks
    gather = 16 * take
    out_id = lax.broadcasted_iota(jnp.int32, (2 * gather, 2 * gather), 0)
    in_id = lax.broadcasted_iota(jnp.int32, (2 * gather, 2 * gather), 1)
    relation_id = out_id // gather
    source = out_id % gather // take
    inner = out_id % take
    place = jnp.where(
        inner < 4,
        relation_id * 64 + source * 4 + inner,
        128 + source * 4 + relation_id * 2 + inner - 4,
    )
    pick = jnp.where(place == in_id, 1.0, 0.0).astype(jnp.bfloat16)
    for block in range(blocks // 16):
        at = slice(block * 16, (block + 1) * 16)
        rows = jnp.concatenate(
            [hidden_ref[at, :, lane * width : (lane + 1) * width].reshape(64, width) for lane in range(3)],
            axis=0,
        )
        ordered = jnp.dot(pick, rows, preferred_element_type=jnp.float32).astype(jnp.bfloat16)
        for relation in range(2):
            start = relation * depth + block * gather
            sorted_ref[start : start + gather, :] = ordered[relation * gather : (relation + 1) * gather]
    out_ref[...] = own_ref[...] + jnp.dot(
        turned_ref[...], sorted_ref[...], preferred_element_type=jnp.float32
    )


VMEM = pl.BlockSpec(memory_space=pltpu.VMEM)
ANY = pl.BlockSpec(memory_space=pl.ANY)
DMA = pltpu.SemaphoreType.DMA
TOKEN = jax.ShapeDtypeStruct((8, 128), jnp.float32)


def vmem_params(mib):
    return pltpu.CompilerParams(vmem_limit_bytes=mib * MIB)


def shards(
    features, rel_weight, self_weight, block_rows, block_cols, count_tiles, live_slots, degrees
):
    width_all, width = features.shape
    relations, slots, block_size, _ = count_tiles.shape
    blocks = lax.axis_size("feat")
    height = width_all // blocks + relations
    send = pl.pallas_call(
        pack_kernel,
        out_shape=jax.ShapeDtypeStruct((blocks, height, width), jnp.bfloat16),
        in_specs=[VMEM, VMEM],
        out_specs=VMEM,
        compiler_params=vmem_params(62),
        name="pack",
    )(features, degrees)
    order = [[FIRST ^ index for index in range(blocks)]]
    panels = lax.all_to_all(
        send, "feat", split_axis=0, concat_axis=0, tiled=True, axis_index_groups=order
    )
    chunks = relations * slots // CHUNK
    tiles, own = pl.pallas_call(
        tiles_kernel,
        out_shape=(
            jax.ShapeDtypeStruct((relations * slots // 2, block_size, 2 * block_size), jnp.int8),
            jax.ShapeDtypeStruct((width_all, width), jnp.float32),
        ),
        in_specs=[ANY, VMEM, VMEM],
        out_specs=(VMEM, VMEM),
        scratch_shapes=[
            pltpu.VMEM((chunks, CHUNK, block_size, block_size), jnp.int32),
            DMA((chunks,)),
        ],
        compiler_params=vmem_params(50),
        cost_estimate=pl.CostEstimate(flops=100_000_000, bytes_accessed=13 * MIB, transcendentals=0),
        name="tiles",
    )(count_tiles, self_weight, features)
    hidden, token = pl.pallas_call(
        slots_kernel,
        out_shape=(jax.ShapeDtypeStruct((blocks, 4, 3 * width), jnp.bfloat16), TOKEN),
        in_specs=[ANY, ANY, ANY, VMEM, VMEM],
        out_specs=(ANY, VMEM),
        scratch_shapes=[
            pltpu.SMEM(block_rows.shape, jnp.int32),
            pltpu.SMEM(block_cols.shape, jnp.int32),
            pltpu.SMEM(live_slots.shape, jnp.int32),
            pltpu.VMEM((relations, blocks, height, width), jnp.float32),
            pltpu.VMEM((blocks, 4, 3 * width), jnp.bfloat16),
            DMA((3,)),
            DMA((PARTS,)),
        ],
        compiler_params=vmem_params(8),
        name="slots",
    )(block_rows, block_cols, live_slots, panels, tiles)
    gathered = lax.all_to_all(
        hidden, "feat", split_axis=0, concat_axis=0, tiled=True, axis_index_groups=order
    )
    turned_weight = pl.pallas_call(
        weights_kernel,
        out_shape=jax.ShapeDtypeStruct((width_all, relations * width_all), jnp.bfloat16),
        in_specs=[VMEM, ANY],
        out_specs=VMEM,
        compiler_params=vmem_params(12),
        cost_estimate=pl.CostEstimate(flops=0, bytes_accessed=5 * MIB, transcendentals=0),
        name="weights",
    )(rel_weight, token)
    partial_sum = pl.pallas_call(
        transform_kernel,
        out_shape=jax.ShapeDtypeStruct((width_all, width), jnp.float32),
        in_specs=[VMEM, VMEM, VMEM],
        out_specs=VMEM,
        scratch_shapes=[pltpu.VMEM((relations * width_all, width), jnp.bfloat16)],
        compiler_params=vmem_params(8),
        name="transform",
    )(turned_weight, gathered, own)
    other = lax.ppermute(partial_sum, "rel", [(0, 1), (1, 0)])
    return jnp.maximum(partial_sum + other, 0.0).astype(jnp.bfloat16)


def solution(mesh):
    placed = (
        P(None, "feat"),
        P("rel", None, None),
        P("rel", None),
        P("rel", None),
        P("rel", None),
        P("rel", None, None, None),
        P("rel"),
        P("rel", "feat"),
    )
    return jax.shard_map(
        shards, mesh=mesh, in_specs=placed, out_specs=P(None, "feat"), check_vma=False
    )
```

```python
import functools

import jax
import jax.numpy as jnp
from jax import lax
from jax.experimental import pallas as pl
from jax.experimental.pallas import tpu as pltpu
from jax.sharding import PartitionSpec as P

GROUP = 32
CHUNK = 8
PARTS = 1
FIRST = 74
PADDED_PAIRS = 80
MIB = 1024 * 1024


def pack_kernel(features_ref, degrees_ref, out_ref):
    blocks, height, width = out_ref.shape
    take = features_ref.shape[0] // blocks
    out_id = lax.broadcasted_iota(jnp.int32, (16 * height, 16 * take), 0)
    in_id = lax.broadcasted_iota(jnp.int32, (16 * height, 16 * take), 1)
    inner = out_id % height
    place = out_id // height * take + inner
    spread = jnp.where((inner < take) & (place == in_id), 1.0, 0.0).astype(jnp.bfloat16)
    row = lax.broadcasted_iota(jnp.int32, (height, width), 0)
    degrees = degrees_ref[...].astype(jnp.float32)
    tail = jnp.where(row == take, degrees[0:1], jnp.where(row == take + 1, degrees[1:2], 0.0))
    for start in range(0, blocks, 16):
        rows = features_ref[start * take : (start + 16) * take, :]
        placed = jnp.dot(spread, rows, preferred_element_type=jnp.float32).reshape(16, height, width)
        out_ref[start : start + 16] = (placed + tail[None]).astype(jnp.bfloat16)


def tiles_kernel(tiles_ref, out_ref, landing_ref, arrived_ref):
    chunks, per_chunk = landing_ref.shape[0], landing_ref.shape[1]
    per_relation = tiles_ref.shape[1] // per_chunk

    def fetch(chunk):
        source = tiles_ref.at[chunk // per_relation, pl.ds(chunk % per_relation * per_chunk, per_chunk)]
        return pltpu.make_async_copy(source, landing_ref.at[chunk], arrived_ref.at[chunk])

    for chunk in range(chunks):
        fetch(chunk).start()

    def turn(chunk, carry):
        fetch(chunk).wait()
        for pair in range(per_chunk // 2):
            turned = [landing_ref[chunk, 2 * pair + side].astype(jnp.float32).T for side in range(2)]
            counts = jnp.concatenate(turned, axis=1).astype(jnp.int32).astype(jnp.int8)
            out_ref[chunk * (per_chunk // 2) + pair] = counts
        return carry

    lax.fori_loop(0, chunks, turn, 0)


def slots_kernel(
    rows_hbm, cols_hbm, live_hbm, panels_ref, tiles_ref, out_ref, token_ref,
    rows_ref, cols_ref, live_ref, sums_ref, done_ref, in_sem, out_sem,
):
    pulls = [
        pltpu.make_async_copy(source, target, in_sem.at[index])
        for index, (source, target) in enumerate(
            ((rows_hbm, rows_ref), (cols_hbm, cols_ref), (live_hbm, live_ref))
        )
    ]
    for pull in pulls:
        pull.start()
    token_ref[...] = jnp.zeros_like(token_ref)
    sums_ref[...] = jnp.zeros_like(sums_ref)
    for pull in pulls:
        pull.wait()
    relations, blocks, height, width = sums_ref.shape
    take = height - relations
    pairs = rows_ref.shape[1] // 2

    def position(block):
        return jnp.bitwise_xor(block, FIRST)

    def add_group(relation, base, live):
        parts = []
        for step in range(0, GROUP, 2):
            slot = base + step
            panel = jnp.concatenate(
                [panels_ref[position(cols_ref[relation, slot + side])] for side in range(2)], axis=0
            )
            tile = tiles_ref[relation * pairs + slot // 2].astype(jnp.bfloat16)
            both = jnp.dot(panel, tile, preferred_element_type=jnp.float32)
            parts += [both[:height, :width], both[height:, width:]]
        for step in range(GROUP):
            slot = base + step
            part = parts[step] if live is None else jnp.where(slot < live, parts[step], 0.0)
            sums_ref[relation, position(rows_ref[relation, slot])] += part

    for relation in range(relations):
        add_group(relation, 0, None)
    for relation in range(relations):
        live = live_ref[relation]
        for base in range(GROUP, rows_ref.shape[1], GROUP):
            pl.when(live > base)(functools.partial(add_group, relation, base, live))

    part_blocks = blocks // PARTS

    def store(part):
        at = pl.ds(part * part_blocks, part_blocks)
        return pltpu.make_async_copy(done_ref.at[at], out_ref.at[at], out_sem.at[part])

    for part in range(PARTS):

        def finish(index, carry, part=part):
            at = pl.ds(part * part_blocks + index * 8, 8)
            packed = panels_ref[at].astype(jnp.float32)
            first, second = [
                sums_ref[relation, at] / packed[:, take + relation : take + relation + 1, :]
                for relation in range(2)
            ]
            rest = jnp.concatenate([first[:, 4:6], second[:, 4:6]], axis=1)
            done_ref[at, :, 0:width] = first[:, 0:4].astype(jnp.bfloat16)
            done_ref[at, :, width : 2 * width] = second[:, 0:4].astype(jnp.bfloat16)
            done_ref[at, :, 2 * width : 3 * width] = rest.astype(jnp.bfloat16)
            return carry

        lax.fori_loop(0, part_blocks // 8, finish, 0)
        store(part).start()
    for part in range(PARTS):
        store(part).wait()


def weights_kernel(rel_ref, self_ref, features_ref, token_ref, turned_ref, own_ref):
    del token_ref
    depth = rel_ref.shape[1]
    take = depth // 128
    gather = 16 * take
    row = lax.broadcasted_iota(jnp.int32, (2 * gather, 2 * gather), 0)
    column = lax.broadcasted_iota(jnp.int32, (2 * gather, 2 * gather), 1)
    third, source, inner = column // 64, column % 64 // 4, column % 4
    relation_id = jnp.where(third < 2, third, inner // 2)
    feature = source * take + jnp.where(third < 2, inner, 4 + inner % 2)
    pick = jnp.where(relation_id * gather + feature == row, 1.0, 0.0).astype(jnp.bfloat16)
    for block in range(8):
        rows = jnp.concatenate(
            [rel_ref[relation, block * gather : (block + 1) * gather, :] for relation in range(2)], axis=0
        )
        moved = lax.dot_general(
            rows, pick, (((0,), (0,)), ((), ())), preferred_element_type=jnp.float32
        ).astype(jnp.bfloat16)
        for lane in range(3):
            start = lane * (2 * depth // 3) + block * 64
            turned_ref[:, start : start + 64] = moved[:, lane * 64 : (lane + 1) * 64]
    half = self_ref.shape[0]
    start = pl.multiple_of(lax.axis_index("rel") * half, half)
    own_ref[...] = lax.dot_general(
        self_ref[...],
        features_ref[pl.ds(start, half), :],
        (((0,), (0,)), ((), ())),
        preferred_element_type=jnp.float32,
    )


def transform_kernel(turned_ref, hidden_ref, own_ref, out_ref):
    blocks = hidden_ref.shape[0]
    width = own_ref.shape[1]
    hidden = jnp.concatenate(
        [hidden_ref[:, :, lane * width : (lane + 1) * width].reshape(4 * blocks, width) for lane in range(3)],
        axis=0,
    )
    out_ref[...] = own_ref[...] + jnp.dot(turned_ref[...], hidden, preferred_element_type=jnp.float32)


VMEM = pl.BlockSpec(memory_space=pltpu.VMEM)
ANY = pl.BlockSpec(memory_space=pl.ANY)
DMA = pltpu.SemaphoreType.DMA
TOKEN = jax.ShapeDtypeStruct((8, 128), jnp.float32)


def vmem_params(mib):
    return pltpu.CompilerParams(vmem_limit_bytes=mib * MIB)


def shards(
    features, rel_weight, self_weight, block_rows, block_cols, count_tiles, live_slots, degrees
):
    width_all, width = features.shape
    relations, slots, block_size, _ = count_tiles.shape
    blocks = lax.axis_size("feat")
    height = width_all // blocks + relations
    send = pl.pallas_call(
        pack_kernel,
        out_shape=jax.ShapeDtypeStruct((blocks, height, width), jnp.bfloat16),
        in_specs=[VMEM, VMEM],
        out_specs=VMEM,
        compiler_params=vmem_params(62),
        name="pack",
    )(features, degrees)
    order = [[FIRST ^ index for index in range(blocks)]]
    panels = lax.all_to_all(
        send, "feat", split_axis=0, concat_axis=0, tiled=True, axis_index_groups=order
    )
    chunks = relations * slots // CHUNK
    tiles = pl.pallas_call(
        tiles_kernel,
        out_shape=jax.ShapeDtypeStruct((PADDED_PAIRS, block_size, 2 * block_size), jnp.int8),
        in_specs=[ANY],
        out_specs=VMEM,
        scratch_shapes=[
            pltpu.VMEM((chunks, CHUNK, block_size, block_size), jnp.int32),
            DMA((chunks,)),
        ],
        compiler_params=vmem_params(50),
        cost_estimate=pl.CostEstimate(flops=0, bytes_accessed=13 * MIB, transcendentals=0),
        name="tiles",
    )(count_tiles)
    hidden, token = pl.pallas_call(
        slots_kernel,
        out_shape=(jax.ShapeDtypeStruct((blocks, 4, 3 * width), jnp.bfloat16), TOKEN),
        in_specs=[ANY, ANY, ANY, VMEM, VMEM],
        out_specs=(ANY, VMEM),
        scratch_shapes=[
            pltpu.SMEM(block_rows.shape, jnp.int32),
            pltpu.SMEM(block_cols.shape, jnp.int32),
            pltpu.SMEM(live_slots.shape, jnp.int32),
            pltpu.VMEM((relations, blocks, height, width), jnp.float32),
            pltpu.VMEM((blocks, 4, 3 * width), jnp.bfloat16),
            DMA((3,)),
            DMA((PARTS,)),
        ],
        compiler_params=vmem_params(8),
        name="slots",
    )(block_rows, block_cols, live_slots, panels, tiles)
    gathered = lax.all_to_all(
        hidden, "feat", split_axis=0, concat_axis=0, tiled=True, axis_index_groups=order
    )
    turned_weight, own = pl.pallas_call(
        weights_kernel,
        out_shape=(
            jax.ShapeDtypeStruct((width_all, relations * width_all), jnp.bfloat16),
            jax.ShapeDtypeStruct((width_all, width), jnp.float32),
        ),
        in_specs=[VMEM, VMEM, VMEM, ANY],
        out_specs=(VMEM, VMEM),
        compiler_params=vmem_params(12),
        cost_estimate=pl.CostEstimate(flops=100_000_000, bytes_accessed=7 * MIB, transcendentals=0),
        name="weights",
    )(rel_weight, self_weight, features, token)
    partial_sum = pl.pallas_call(
        transform_kernel,
        out_shape=jax.ShapeDtypeStruct((width_all, width), jnp.float32),
        in_specs=[VMEM, VMEM, VMEM],
        out_specs=VMEM,
        compiler_params=vmem_params(8),
        name="transform",
    )(turned_weight, gathered, own)
    other = lax.ppermute(partial_sum, "rel", [(0, 1), (1, 0)])
    return jnp.maximum(partial_sum + other, 0.0).astype(jnp.bfloat16)


def solution(mesh):
    placed = (
        P(None, "feat"),
        P("rel", None, None),
        P("rel", None),
        P("rel", None),
        P("rel", None),
        P("rel", None, None, None),
        P("rel"),
        P("rel", "feat"),
    )
    return jax.shard_map(
        shards, mesh=mesh, in_specs=placed, out_specs=P(None, "feat"), check_vma=False
    )
```

```python
import functools

import jax
import jax.numpy as jnp
from jax import lax
from jax.experimental import pallas as pl
from jax.experimental.pallas import tpu as pltpu
from jax.sharding import PartitionSpec as P

GROUP = 32
CHUNK = 8
PARTS = 2
FIRST = 90
PADDED_PAIRS = 80
MIB = 1024 * 1024


def pack_kernel(features_ref, degrees_ref, out_ref):
    blocks, height, width = out_ref.shape
    take = features_ref.shape[0] // blocks
    out_id = lax.broadcasted_iota(jnp.int32, (16 * height, 16 * take), 0)
    in_id = lax.broadcasted_iota(jnp.int32, (16 * height, 16 * take), 1)
    inner = out_id % height
    place = out_id // height * take + inner
    spread = jnp.where((inner < take) & (place == in_id), 1.0, 0.0).astype(jnp.bfloat16)
    row = lax.broadcasted_iota(jnp.int32, (height, width), 0)
    degrees = degrees_ref[...].astype(jnp.float32)
    tail = jnp.where(row == take, degrees[0:1], jnp.where(row == take + 1, degrees[1:2], 0.0))
    for start in range(0, blocks, 16):
        rows = features_ref[start * take : (start + 16) * take, :]
        placed = jnp.dot(spread, rows, preferred_element_type=jnp.float32).reshape(16, height, width)
        out_ref[start : start + 16] = (placed + tail[None]).astype(jnp.bfloat16)


def hops(block, other):
    total = 0
    for size, stride in ((8, 16), (4, 4), (4, 1)):
        apart = abs(block // stride % size - other // stride % size)
        total += min(apart, size - apart)
    return total


def block_order(blocks):
    rest = [block for block in range(blocks) if block != FIRST]
    return [FIRST] + sorted(rest, key=lambda block: (-hops(block, FIRST), block))


def positions(block, order):
    found = jnp.zeros_like(block)
    for index, member in enumerate(order):
        found = jnp.where(block == member, index, found)
    return found


def tiles_kernel(tiles_ref, rows_ref, cols_ref, out_ref, row_at_ref, col_at_ref, landing_ref, arrived_ref):
    chunks, per_chunk = landing_ref.shape[0], landing_ref.shape[1]
    per_relation = tiles_ref.shape[1] // per_chunk

    def fetch(chunk):
        source = tiles_ref.at[chunk // per_relation, pl.ds(chunk % per_relation * per_chunk, per_chunk)]
        return pltpu.make_async_copy(source, landing_ref.at[chunk], arrived_ref.at[chunk])

    for chunk in range(chunks):
        fetch(chunk).start()
    order = block_order(128)
    row_at_ref[...] = positions(rows_ref[...], order)
    col_at_ref[...] = positions(cols_ref[...], order)

    def turn(chunk, carry):
        fetch(chunk).wait()
        for pair in range(per_chunk // 2):
            turned = [landing_ref[chunk, 2 * pair + side].astype(jnp.float32).T for side in range(2)]
            counts = jnp.concatenate(turned, axis=1).astype(jnp.int32).astype(jnp.int8)
            out_ref[chunk * (per_chunk // 2) + pair] = counts
        return carry

    lax.fori_loop(0, chunks, turn, 0)


def slots_kernel(
    rows_hbm, cols_hbm, live_hbm, panels_ref, tiles_ref, out_ref, token_ref,
    rows_ref, cols_ref, live_ref, sums_ref, done_ref, in_sem, out_sem,
):
    pulls = [
        pltpu.make_async_copy(source, target, in_sem.at[index])
        for index, (source, target) in enumerate(
            ((rows_hbm, rows_ref), (cols_hbm, cols_ref), (live_hbm, live_ref))
        )
    ]
    for pull in pulls:
        pull.start()
    token_ref[...] = jnp.zeros_like(token_ref)
    sums_ref[...] = jnp.zeros_like(sums_ref)
    for pull in pulls:
        pull.wait()
    relations, blocks, height, width = sums_ref.shape
    take = height - relations
    pairs = rows_ref.shape[1] // 2

    def add_group(relation, base, live):
        parts = []
        for step in range(0, GROUP, 2):
            slot = base + step
            panel = jnp.concatenate(
                [panels_ref[cols_ref[relation, slot + side]] for side in range(2)], axis=0
            )
            tile = tiles_ref[relation * pairs + slot // 2].astype(jnp.bfloat16)
            both = jnp.dot(panel, tile, preferred_element_type=jnp.float32)
            parts += [both[:height, :width], both[height:, width:]]
        for step in range(GROUP):
            slot = base + step
            part = parts[step] if live is None else jnp.where(slot < live, parts[step], 0.0)
            sums_ref[relation, rows_ref[relation, slot]] += part

    for relation in range(relations):
        add_group(relation, 0, None)
    for relation in range(relations):
        live = live_ref[relation]
        for base in range(GROUP, rows_ref.shape[1], GROUP):
            pl.when(live > base)(functools.partial(add_group, relation, base, live))

    part_blocks = blocks // PARTS

    def store(part):
        at = pl.ds(part * part_blocks, part_blocks)
        return pltpu.make_async_copy(done_ref.at[at], out_ref.at[at], out_sem.at[part])

    for part in range(PARTS):

        def finish(index, carry, part=part):
            at = pl.ds(part * part_blocks + index * 8, 8)
            packed = panels_ref[at].astype(jnp.float32)
            first, second = [
                sums_ref[relation, at] / packed[:, take + relation : take + relation + 1, :]
                for relation in range(2)
            ]
            rest = jnp.concatenate([first[:, 4:6], second[:, 4:6]], axis=1)
            done_ref[at, :, 0:width] = first[:, 0:4].astype(jnp.bfloat16)
            done_ref[at, :, width : 2 * width] = second[:, 0:4].astype(jnp.bfloat16)
            done_ref[at, :, 2 * width : 3 * width] = rest.astype(jnp.bfloat16)
            return carry

        lax.fori_loop(0, part_blocks // 8, finish, 0, unroll=4)
        store(part).start()
    for part in range(PARTS):
        store(part).wait()


def weights_kernel(rel_ref, self_ref, features_ref, token_ref, turned_ref, own_ref):
    del token_ref
    depth = rel_ref.shape[1]
    take = depth // 128
    gather = 16 * take
    row = lax.broadcasted_iota(jnp.int32, (2 * gather, 2 * gather), 0)
    column = lax.broadcasted_iota(jnp.int32, (2 * gather, 2 * gather), 1)
    third, source, inner = column // 64, column % 64 // 4, column % 4
    relation_id = jnp.where(third < 2, third, inner // 2)
    feature = source * take + jnp.where(third < 2, inner, 4 + inner % 2)
    pick = jnp.where(relation_id * gather + feature == row, 1.0, 0.0).astype(jnp.bfloat16)
    for block in range(8):
        rows = jnp.concatenate(
            [rel_ref[relation, block * gather : (block + 1) * gather, :] for relation in range(2)], axis=0
        )
        moved = lax.dot_general(
            rows, pick, (((0,), (0,)), ((), ())), preferred_element_type=jnp.float32
        ).astype(jnp.bfloat16)
        for lane in range(3):
            start = lane * (2 * depth // 3) + block * 64
            turned_ref[:, start : start + 64] = moved[:, lane * 64 : (lane + 1) * 64]
    half = self_ref.shape[0]
    start = pl.multiple_of(lax.axis_index("rel") * half, half)
    own_ref[...] = lax.dot_general(
        self_ref[...],
        features_ref[pl.ds(start, half), :],
        (((0,), (0,)), ((), ())),
        preferred_element_type=jnp.float32,
    )


def transform_kernel(turned_ref, hidden_ref, own_ref, out_ref):
    blocks = hidden_ref.shape[0]
    width = own_ref.shape[1]
    hidden = jnp.concatenate(
        [hidden_ref[:, :, lane * width : (lane + 1) * width].reshape(4 * blocks, width) for lane in range(3)],
        axis=0,
    )
    out_ref[...] = own_ref[...] + jnp.dot(turned_ref[...], hidden, preferred_element_type=jnp.float32)


VMEM = pl.BlockSpec(memory_space=pltpu.VMEM)
ANY = pl.BlockSpec(memory_space=pl.ANY)
DMA = pltpu.SemaphoreType.DMA
TOKEN = jax.ShapeDtypeStruct((8, 128), jnp.float32)


def vmem_params(mib):
    return pltpu.CompilerParams(vmem_limit_bytes=mib * MIB)


def shards(
    features, rel_weight, self_weight, block_rows, block_cols, count_tiles, live_slots, degrees
):
    width_all, width = features.shape
    relations, slots, block_size, _ = count_tiles.shape
    blocks = lax.axis_size("feat")
    height = width_all // blocks + relations
    send = pl.pallas_call(
        pack_kernel,
        out_shape=jax.ShapeDtypeStruct((blocks, height, width), jnp.bfloat16),
        in_specs=[VMEM, VMEM],
        out_specs=VMEM,
        compiler_params=vmem_params(62),
        name="pack",
    )(features, degrees)
    order = [block_order(blocks)]
    panels = lax.all_to_all(
        send, "feat", split_axis=0, concat_axis=0, tiled=True, axis_index_groups=order
    )
    chunks = relations * slots // CHUNK
    tiles, row_at, col_at = pl.pallas_call(
        tiles_kernel,
        out_shape=(
            jax.ShapeDtypeStruct((PADDED_PAIRS, block_size, 2 * block_size), jnp.int8),
            jax.ShapeDtypeStruct(block_rows.shape, jnp.int32),
            jax.ShapeDtypeStruct(block_cols.shape, jnp.int32),
        ),
        in_specs=[ANY, VMEM, VMEM],
        out_specs=(VMEM, VMEM, VMEM),
        scratch_shapes=[
            pltpu.VMEM((chunks, CHUNK, block_size, block_size), jnp.int32),
            DMA((chunks,)),
        ],
        compiler_params=vmem_params(50),
        cost_estimate=pl.CostEstimate(flops=0, bytes_accessed=13 * MIB, transcendentals=0),
        name="tiles",
    )(count_tiles, block_rows, block_cols)
    hidden, token = pl.pallas_call(
        slots_kernel,
        out_shape=(jax.ShapeDtypeStruct((blocks, 4, 3 * width), jnp.bfloat16), TOKEN),
        in_specs=[ANY, ANY, ANY, VMEM, VMEM],
        out_specs=(ANY, VMEM),
        scratch_shapes=[
            pltpu.SMEM(block_rows.shape, jnp.int32),
            pltpu.SMEM(block_cols.shape, jnp.int32),
            pltpu.SMEM(live_slots.shape, jnp.int32),
            pltpu.VMEM((relations, blocks, height, width), jnp.float32),
            pltpu.VMEM((blocks, 4, 3 * width), jnp.bfloat16),
            DMA((3,)),
            DMA((PARTS,)),
        ],
        compiler_params=vmem_params(8),
        name="slots",
    )(row_at, col_at, live_slots, panels, tiles)
    gathered = lax.all_to_all(
        hidden, "feat", split_axis=0, concat_axis=0, tiled=True, axis_index_groups=order
    )
    turned_weight, own = pl.pallas_call(
        weights_kernel,
        out_shape=(
            jax.ShapeDtypeStruct((width_all, relations * width_all), jnp.bfloat16),
            jax.ShapeDtypeStruct((width_all, width), jnp.float32),
        ),
        in_specs=[VMEM, VMEM, VMEM, ANY],
        out_specs=(VMEM, VMEM),
        compiler_params=vmem_params(12),
        cost_estimate=pl.CostEstimate(flops=100_000_000, bytes_accessed=7 * MIB, transcendentals=0),
        name="weights",
    )(rel_weight, self_weight, features, token)
    partial_sum = pl.pallas_call(
        transform_kernel,
        out_shape=jax.ShapeDtypeStruct((width_all, width), jnp.float32),
        in_specs=[VMEM, VMEM, VMEM],
        out_specs=VMEM,
        compiler_params=vmem_params(8),
        name="transform",
    )(turned_weight, gathered, own)
    other = lax.ppermute(partial_sum, "rel", [(0, 1), (1, 0)])
    return jnp.maximum(partial_sum + other, 0.0).astype(jnp.bfloat16)


def solution(mesh):
    placed = (
        P(None, "feat"),
        P("rel", None, None),
        P("rel", None),
        P("rel", None),
        P("rel", None),
        P("rel", None, None, None),
        P("rel"),
        P("rel", "feat"),
    )
    return jax.shard_map(
        shards, mesh=mesh, in_specs=placed, out_specs=P(None, "feat"), check_vma=False
    )
```

```python
import functools

import jax
import jax.numpy as jnp
from jax import lax
from jax.experimental import pallas as pl
from jax.experimental.pallas import tpu as pltpu
from jax.sharding import PartitionSpec as P

GROUP = 32
CHUNK = 8
PARTS = 2
FIRST = 90
PADDED_PAIRS = 80
MIB = 1024 * 1024


def pack_kernel(features_ref, degrees_ref, out_ref):
    blocks, height, width = out_ref.shape
    take = features_ref.shape[0] // blocks
    out_id = lax.broadcasted_iota(jnp.int32, (16 * height, 16 * take), 0)
    in_id = lax.broadcasted_iota(jnp.int32, (16 * height, 16 * take), 1)
    inner = out_id % height
    place = out_id // height * take + inner
    spread = jnp.where((inner < take) & (place == in_id), 1.0, 0.0).astype(jnp.bfloat16)
    row = lax.broadcasted_iota(jnp.int32, (height, width), 0)
    degrees = degrees_ref[...].astype(jnp.float32)
    tail = jnp.where(row == take, degrees[0:1], jnp.where(row == take + 1, degrees[1:2], 0.0))
    for start in range(0, blocks, 16):
        rows = features_ref[start * take : (start + 16) * take, :]
        placed = jnp.dot(spread, rows, preferred_element_type=jnp.float32).reshape(16, height, width)
        out_ref[start : start + 16] = (placed + tail[None]).astype(jnp.bfloat16)


def hops(block, other):
    total = 0
    for size, stride in ((8, 16), (4, 4), (4, 1)):
        apart = abs(block // stride % size - other // stride % size)
        total += min(apart, size - apart)
    return total


def block_order(blocks):
    rest = [block for block in range(blocks) if block != FIRST]
    return [FIRST] + sorted(rest, key=lambda block: (-hops(block, FIRST), block))


def positions(block, order):
    found = jnp.zeros_like(block)
    for index, member in enumerate(order):
        found = jnp.where(block == member, index, found)
    return found


def tiles_kernel(tiles_ref, rows_ref, cols_ref, out_ref, row_at_ref, col_at_ref, landing_ref, arrived_ref):
    chunks, per_chunk = landing_ref.shape[0], landing_ref.shape[1]
    per_relation = tiles_ref.shape[1] // per_chunk

    def fetch(chunk):
        source = tiles_ref.at[chunk // per_relation, pl.ds(chunk % per_relation * per_chunk, per_chunk)]
        return pltpu.make_async_copy(source, landing_ref.at[chunk], arrived_ref.at[chunk])

    for chunk in range(chunks):
        fetch(chunk).start()
    order = block_order(128)
    row_at_ref[...] = positions(rows_ref[...], order)
    col_at_ref[...] = positions(cols_ref[...], order)

    def turn(chunk, carry):
        fetch(chunk).wait()
        for pair in range(per_chunk // 2):
            turned = [landing_ref[chunk, 2 * pair + side].astype(jnp.float32).T for side in range(2)]
            counts = jnp.concatenate(turned, axis=1).astype(jnp.int32).astype(jnp.int8)
            out_ref[chunk * (per_chunk // 2) + pair] = counts
        return carry

    lax.fori_loop(0, chunks, turn, 0)


def slots_kernel(
    rows_hbm, cols_hbm, live_hbm, panels_ref, tiles_ref, out_ref, token_ref,
    rows_ref, cols_ref, live_ref, inverse_ref, sums_ref, done_ref, in_sem, out_sem,
):
    pulls = [
        pltpu.make_async_copy(source, target, in_sem.at[index])
        for index, (source, target) in enumerate(
            ((rows_hbm, rows_ref), (cols_hbm, cols_ref), (live_hbm, live_ref))
        )
    ]
    for pull in pulls:
        pull.start()
    token_ref[...] = jnp.zeros_like(token_ref)
    sums_ref[...] = jnp.zeros_like(sums_ref)
    relations, blocks, height, width = sums_ref.shape
    take = height - relations
    inverse_ref[...] = 1.0 / panels_ref[:, take:height, :].astype(jnp.float32)
    for pull in pulls:
        pull.wait()
    pairs = rows_ref.shape[1] // 2

    def add_group(relation, base, live):
        parts = []
        for step in range(0, GROUP, 2):
            slot = base + step
            panel = jnp.concatenate(
                [panels_ref[cols_ref[relation, slot + side]] for side in range(2)], axis=0
            )
            tile = tiles_ref[relation * pairs + slot // 2].astype(jnp.bfloat16)
            both = jnp.dot(panel, tile, preferred_element_type=jnp.float32)
            parts += [both[:height, :width], both[height:, width:]]
        for step in range(GROUP):
            slot = base + step
            part = parts[step] if live is None else jnp.where(slot < live, parts[step], 0.0)
            sums_ref[relation, rows_ref[relation, slot]] += part

    for relation in range(relations):
        add_group(relation, 0, None)
    for relation in range(relations):
        live = live_ref[relation]
        for base in range(GROUP, rows_ref.shape[1], GROUP):
            pl.when(live > base)(functools.partial(add_group, relation, base, live))

    part_blocks = blocks // PARTS

    def store(part):
        at = pl.ds(part * part_blocks, part_blocks)
        return pltpu.make_async_copy(done_ref.at[at], out_ref.at[at], out_sem.at[part])

    for part in range(PARTS):

        def finish(index, carry, part=part):
            at = pl.ds(part * part_blocks + index * 8, 8)
            inverse = inverse_ref[at]
            first, second = [
                sums_ref[relation, at] * inverse[:, relation : relation + 1, :]
                for relation in range(2)
            ]
            rest = jnp.concatenate([first[:, 4:6], second[:, 4:6]], axis=1)
            done_ref[at, :, 0:width] = first[:, 0:4].astype(jnp.bfloat16)
            done_ref[at, :, width : 2 * width] = second[:, 0:4].astype(jnp.bfloat16)
            done_ref[at, :, 2 * width : 3 * width] = rest.astype(jnp.bfloat16)
            return carry

        lax.fori_loop(0, part_blocks // 8, finish, 0, unroll=4)
        store(part).start()
    for part in range(PARTS):
        store(part).wait()


def weights_kernel(rel_ref, self_ref, features_ref, token_ref, turned_ref, own_ref):
    del token_ref
    depth = rel_ref.shape[1]
    take = depth // 128
    gather = 16 * take
    row = lax.broadcasted_iota(jnp.int32, (2 * gather, 2 * gather), 0)
    column = lax.broadcasted_iota(jnp.int32, (2 * gather, 2 * gather), 1)
    third, source, inner = column // 64, column % 64 // 4, column % 4
    relation_id = jnp.where(third < 2, third, inner // 2)
    feature = source * take + jnp.where(third < 2, inner, 4 + inner % 2)
    pick = jnp.where(relation_id * gather + feature == row, 1.0, 0.0).astype(jnp.bfloat16)
    for block in range(8):
        rows = jnp.concatenate(
            [rel_ref[relation, block * gather : (block + 1) * gather, :] for relation in range(2)], axis=0
        )
        moved = lax.dot_general(
            rows, pick, (((0,), (0,)), ((), ())), preferred_element_type=jnp.float32
        ).astype(jnp.bfloat16)
        for lane in range(3):
            start = lane * (2 * depth // 3) + block * 64
            turned_ref[:, start : start + 64] = moved[:, lane * 64 : (lane + 1) * 64]
    half = self_ref.shape[0]
    start = pl.multiple_of(lax.axis_index("rel") * half, half)
    own_ref[...] = lax.dot_general(
        self_ref[...],
        features_ref[pl.ds(start, half), :],
        (((0,), (0,)), ((), ())),
        preferred_element_type=jnp.float32,
    )


def transform_kernel(turned_ref, hidden_ref, own_ref, out_ref):
    blocks = hidden_ref.shape[0]
    width = own_ref.shape[1]
    hidden = jnp.concatenate(
        [hidden_ref[:, :, lane * width : (lane + 1) * width].reshape(4 * blocks, width) for lane in range(3)],
        axis=0,
    )
    out_ref[...] = own_ref[...] + jnp.dot(turned_ref[...], hidden, preferred_element_type=jnp.float32)


VMEM = pl.BlockSpec(memory_space=pltpu.VMEM)
ANY = pl.BlockSpec(memory_space=pl.ANY)
DMA = pltpu.SemaphoreType.DMA
TOKEN = jax.ShapeDtypeStruct((8, 128), jnp.float32)


def vmem_params(mib):
    return pltpu.CompilerParams(vmem_limit_bytes=mib * MIB)


def shards(
    features, rel_weight, self_weight, block_rows, block_cols, count_tiles, live_slots, degrees
):
    width_all, width = features.shape
    relations, slots, block_size, _ = count_tiles.shape
    blocks = lax.axis_size("feat")
    height = width_all // blocks + relations
    send = pl.pallas_call(
        pack_kernel,
        out_shape=jax.ShapeDtypeStruct((blocks, height, width), jnp.bfloat16),
        in_specs=[VMEM, VMEM],
        out_specs=VMEM,
        compiler_params=vmem_params(62),
        name="pack",
    )(features, degrees)
    order = [block_order(blocks)]
    panels = lax.all_to_all(
        send, "feat", split_axis=0, concat_axis=0, tiled=True, axis_index_groups=order
    )
    chunks = relations * slots // CHUNK
    tiles, row_at, col_at = pl.pallas_call(
        tiles_kernel,
        out_shape=(
            jax.ShapeDtypeStruct((PADDED_PAIRS, block_size, 2 * block_size), jnp.int8),
            jax.ShapeDtypeStruct(block_rows.shape, jnp.int32),
            jax.ShapeDtypeStruct(block_cols.shape, jnp.int32),
        ),
        in_specs=[ANY, VMEM, VMEM],
        out_specs=(VMEM, VMEM, VMEM),
        scratch_shapes=[
            pltpu.VMEM((chunks, CHUNK, block_size, block_size), jnp.int32),
            DMA((chunks,)),
        ],
        compiler_params=vmem_params(50),
        cost_estimate=pl.CostEstimate(flops=0, bytes_accessed=13 * MIB, transcendentals=0),
        name="tiles",
    )(count_tiles, block_rows, block_cols)
    hidden, token = pl.pallas_call(
        slots_kernel,
        out_shape=(jax.ShapeDtypeStruct((blocks, 4, 3 * width), jnp.bfloat16), TOKEN),
        in_specs=[ANY, ANY, ANY, VMEM, VMEM],
        out_specs=(ANY, VMEM),
        scratch_shapes=[
            pltpu.SMEM(block_rows.shape, jnp.int32),
            pltpu.SMEM(block_cols.shape, jnp.int32),
            pltpu.SMEM(live_slots.shape, jnp.int32),
            pltpu.VMEM((blocks, relations, width), jnp.float32),
            pltpu.VMEM((relations, blocks, height, width), jnp.float32),
            pltpu.VMEM((blocks, 4, 3 * width), jnp.bfloat16),
            DMA((3,)),
            DMA((PARTS,)),
        ],
        compiler_params=vmem_params(8),
        name="slots",
    )(row_at, col_at, live_slots, panels, tiles)
    gathered = lax.all_to_all(
        hidden, "feat", split_axis=0, concat_axis=0, tiled=True, axis_index_groups=order
    )
    turned_weight, own = pl.pallas_call(
        weights_kernel,
        out_shape=(
            jax.ShapeDtypeStruct((width_all, relations * width_all), jnp.bfloat16),
            jax.ShapeDtypeStruct((width_all, width), jnp.float32),
        ),
        in_specs=[VMEM, VMEM, VMEM, ANY],
        out_specs=(VMEM, VMEM),
        compiler_params=vmem_params(12),
        cost_estimate=pl.CostEstimate(flops=100_000_000, bytes_accessed=7 * MIB, transcendentals=0),
        name="weights",
    )(rel_weight, self_weight, features, token)
    partial_sum = pl.pallas_call(
        transform_kernel,
        out_shape=jax.ShapeDtypeStruct((width_all, width), jnp.float32),
        in_specs=[VMEM, VMEM, VMEM],
        out_specs=VMEM,
        compiler_params=vmem_params(8),
        name="transform",
    )(turned_weight, gathered, own)
    other = lax.ppermute(partial_sum, "rel", [(0, 1), (1, 0)])
    return jnp.maximum(partial_sum + other, 0.0).astype(jnp.bfloat16)


def solution(mesh):
    placed = (
        P(None, "feat"),
        P("rel", None, None),
        P("rel", None),
        P("rel", None),
        P("rel", None),
        P("rel", None, None, None),
        P("rel"),
        P("rel", "feat"),
    )
    return jax.shard_map(
        shards, mesh=mesh, in_specs=placed, out_specs=P(None, "feat"), check_vma=False
    )
```

```python
import functools

import jax
import jax.numpy as jnp
from jax import lax
from jax.experimental import pallas as pl
from jax.experimental.pallas import tpu as pltpu
from jax.sharding import PartitionSpec as P

GROUP = 32
CHUNK = 8
PARTS = 2
FIRST = 90
PADDED_PAIRS = 80
MIB = 1024 * 1024


def pack_kernel(features_ref, degrees_ref, out_ref):
    blocks, height, width = out_ref.shape
    take = features_ref.shape[0] // blocks
    out_id = lax.broadcasted_iota(jnp.int32, (16 * height, 16 * take), 0)
    in_id = lax.broadcasted_iota(jnp.int32, (16 * height, 16 * take), 1)
    inner = out_id % height
    place = out_id // height * take + inner
    spread = jnp.where((inner < take) & (place == in_id), 1.0, 0.0).astype(jnp.bfloat16)
    row = lax.broadcasted_iota(jnp.int32, (height, width), 0)
    degrees = degrees_ref[...].astype(jnp.float32)
    tail = jnp.where(row == take, degrees[0:1], jnp.where(row == take + 1, degrees[1:2], 0.0))
    for start in range(0, blocks, 16):
        rows = features_ref[start * take : (start + 16) * take, :]
        placed = jnp.dot(spread, rows, preferred_element_type=jnp.float32).reshape(16, height, width)
        out_ref[start : start + 16] = (placed + tail[None]).astype(jnp.bfloat16)


def hops(block, other):
    total = 0
    for size, stride in ((8, 16), (4, 4), (4, 1)):
        apart = abs(block // stride % size - other // stride % size)
        total += min(apart, size - apart)
    return total


def block_order(blocks):
    rest = [block for block in range(blocks) if block != FIRST]
    return [FIRST] + sorted(rest, key=lambda block: (-hops(block, FIRST), block))


def positions(block, order):
    found = jnp.zeros_like(block)
    for index, member in enumerate(order):
        found = jnp.where(block == member, index, found)
    return found


def tiles_kernel(tiles_ref, rows_ref, cols_ref, out_ref, row_at_ref, col_at_ref, landing_ref, arrived_ref):
    chunks, per_chunk = landing_ref.shape[0], landing_ref.shape[1]
    per_relation = tiles_ref.shape[1] // per_chunk

    def fetch(chunk):
        source = tiles_ref.at[chunk // per_relation, pl.ds(chunk % per_relation * per_chunk, per_chunk)]
        return pltpu.make_async_copy(source, landing_ref.at[chunk], arrived_ref.at[chunk])

    for chunk in range(chunks):
        fetch(chunk).start()
    order = block_order(128)
    row_at_ref[...] = positions(rows_ref[...], order)
    col_at_ref[...] = positions(cols_ref[...], order)

    def turn(chunk, carry):
        fetch(chunk).wait()
        for pair in range(per_chunk // 2):
            turned = [landing_ref[chunk, 2 * pair + side].astype(jnp.float32).T for side in range(2)]
            counts = jnp.concatenate(turned, axis=1).astype(jnp.int32).astype(jnp.int8)
            out_ref[chunk * (per_chunk // 2) + pair] = counts
        return carry

    lax.fori_loop(0, chunks, turn, 0)


def slots_kernel(
    rows_hbm, cols_hbm, live_hbm, panels_ref, tiles_ref, out_ref, token_ref,
    rows_ref, cols_ref, live_ref, inverse_ref, sums_ref, done_ref, in_sem, out_sem,
):
    pulls = [
        pltpu.make_async_copy(source, target, in_sem.at[index])
        for index, (source, target) in enumerate(
            ((rows_hbm, rows_ref), (cols_hbm, cols_ref), (live_hbm, live_ref))
        )
    ]
    for pull in pulls:
        pull.start()
    token_ref[...] = jnp.zeros_like(token_ref)
    sums_ref[...] = jnp.zeros_like(sums_ref)
    relations, blocks, height, width = sums_ref.shape
    take = height - relations
    inverse_ref[...] = 1.0 / panels_ref[:, take:height, :].astype(jnp.float32)
    for pull in pulls:
        pull.wait()
    pairs = rows_ref.shape[1] // 2

    def add_group(relation, base, live):
        parts = []
        for step in range(0, GROUP, 2):
            slot = base + step
            panel = jnp.concatenate(
                [panels_ref[cols_ref[relation, slot + side]] for side in range(2)], axis=0
            )
            tile = tiles_ref[relation * pairs + slot // 2].astype(jnp.bfloat16)
            both = jnp.dot(panel, tile, preferred_element_type=jnp.float32)
            parts += [both[:height, :width], both[height:, width:]]
        for step in range(GROUP):
            slot = base + step
            part = parts[step] if live is None else jnp.where(slot < live, parts[step], 0.0)
            sums_ref[relation, rows_ref[relation, slot]] += part

    for relation in range(relations):
        add_group(relation, 0, None)
    for relation in range(relations):
        live = live_ref[relation]
        for base in range(GROUP, rows_ref.shape[1], GROUP):
            pl.when(live > base)(functools.partial(add_group, relation, base, live))

    part_blocks = blocks // PARTS

    def store(part):
        at = pl.ds(part * part_blocks, part_blocks)
        return pltpu.make_async_copy(done_ref.at[at], out_ref.at[at], out_sem.at[part])

    for part in range(PARTS):

        def finish(index, carry, part=part):
            at = pl.ds(part * part_blocks + index * 8, 8)
            inverse = inverse_ref[at]
            first, second = [
                sums_ref[relation, at] * inverse[:, relation : relation + 1, :]
                for relation in range(2)
            ]
            rest = jnp.concatenate([first[:, 4:6], second[:, 4:6]], axis=1)
            done_ref[at, :, 0:width] = first[:, 0:4].astype(jnp.bfloat16)
            done_ref[at, :, width : 2 * width] = second[:, 0:4].astype(jnp.bfloat16)
            done_ref[at, :, 2 * width : 3 * width] = rest.astype(jnp.bfloat16)
            return carry

        lax.fori_loop(0, part_blocks // 8, finish, 0, unroll=8)
        store(part).start()
    for part in range(PARTS):
        store(part).wait()


def weights_kernel(rel_ref, self_ref, features_ref, token_ref, turned_ref, own_ref):
    del token_ref
    depth = rel_ref.shape[1]
    take = depth // 128
    gather = 16 * take
    row = lax.broadcasted_iota(jnp.int32, (2 * gather, 2 * gather), 0)
    column = lax.broadcasted_iota(jnp.int32, (2 * gather, 2 * gather), 1)
    third, source, inner = column // 64, column % 64 // 4, column % 4
    relation_id = jnp.where(third < 2, third, inner // 2)
    feature = source * take + jnp.where(third < 2, inner, 4 + inner % 2)
    pick = jnp.where(relation_id * gather + feature == row, 1.0, 0.0).astype(jnp.bfloat16)
    for block in range(8):
        rows = jnp.concatenate(
            [rel_ref[relation, block * gather : (block + 1) * gather, :] for relation in range(2)], axis=0
        )
        moved = lax.dot_general(
            rows, pick, (((0,), (0,)), ((), ())), preferred_element_type=jnp.float32
        ).astype(jnp.bfloat16)
        for lane in range(3):
            start = lane * (2 * depth // 3) + block * 64
            turned_ref[:, start : start + 64] = moved[:, lane * 64 : (lane + 1) * 64]
    half = self_ref.shape[0]
    start = pl.multiple_of(lax.axis_index("rel") * half, half)
    own_ref[...] = lax.dot_general(
        self_ref[...],
        features_ref[pl.ds(start, half), :],
        (((0,), (0,)), ((), ())),
        preferred_element_type=jnp.float32,
    )


def transform_kernel(turned_ref, hidden_ref, own_ref, out_ref):
    blocks = hidden_ref.shape[0]
    width = own_ref.shape[1]
    hidden = jnp.concatenate(
        [hidden_ref[:, :, lane * width : (lane + 1) * width].reshape(4 * blocks, width) for lane in range(3)],
        axis=0,
    )
    out_ref[...] = own_ref[...] + jnp.dot(turned_ref[...], hidden, preferred_element_type=jnp.float32)


VMEM = pl.BlockSpec(memory_space=pltpu.VMEM)
ANY = pl.BlockSpec(memory_space=pl.ANY)
DMA = pltpu.SemaphoreType.DMA
TOKEN = jax.ShapeDtypeStruct((8, 128), jnp.float32)


def vmem_params(mib):
    return pltpu.CompilerParams(vmem_limit_bytes=mib * MIB)


def shards(
    features, rel_weight, self_weight, block_rows, block_cols, count_tiles, live_slots, degrees
):
    width_all, width = features.shape
    relations, slots, block_size, _ = count_tiles.shape
    blocks = lax.axis_size("feat")
    height = width_all // blocks + relations
    send = pl.pallas_call(
        pack_kernel,
        out_shape=jax.ShapeDtypeStruct((blocks, height, width), jnp.bfloat16),
        in_specs=[VMEM, VMEM],
        out_specs=VMEM,
        compiler_params=vmem_params(62),
        name="pack",
    )(features, degrees)
    order = [block_order(blocks)]
    panels = lax.all_to_all(
        send, "feat", split_axis=0, concat_axis=0, tiled=True, axis_index_groups=order
    )
    chunks = relations * slots // CHUNK
    tiles, row_at, col_at = pl.pallas_call(
        tiles_kernel,
        out_shape=(
            jax.ShapeDtypeStruct((PADDED_PAIRS, block_size, 2 * block_size), jnp.int8),
            jax.ShapeDtypeStruct(block_rows.shape, jnp.int32),
            jax.ShapeDtypeStruct(block_cols.shape, jnp.int32),
        ),
        in_specs=[ANY, VMEM, VMEM],
        out_specs=(VMEM, VMEM, VMEM),
        scratch_shapes=[
            pltpu.VMEM((chunks, CHUNK, block_size, block_size), jnp.int32),
            DMA((chunks,)),
        ],
        compiler_params=vmem_params(50),
        cost_estimate=pl.CostEstimate(flops=0, bytes_accessed=13 * MIB, transcendentals=0),
        name="tiles",
    )(count_tiles, block_rows, block_cols)
    hidden, token = pl.pallas_call(
        slots_kernel,
        out_shape=(jax.ShapeDtypeStruct((blocks, 4, 3 * width), jnp.bfloat16), TOKEN),
        in_specs=[ANY, ANY, ANY, VMEM, VMEM],
        out_specs=(ANY, VMEM),
        scratch_shapes=[
            pltpu.SMEM(block_rows.shape, jnp.int32),
            pltpu.SMEM(block_cols.shape, jnp.int32),
            pltpu.SMEM(live_slots.shape, jnp.int32),
            pltpu.VMEM((blocks, relations, width), jnp.float32),
            pltpu.VMEM((relations, blocks, height, width), jnp.float32),
            pltpu.VMEM((blocks, 4, 3 * width), jnp.bfloat16),
            DMA((3,)),
            DMA((PARTS,)),
        ],
        compiler_params=vmem_params(8),
        name="slots",
    )(row_at, col_at, live_slots, panels, tiles)
    gathered = lax.all_to_all(
        hidden, "feat", split_axis=0, concat_axis=0, tiled=True, axis_index_groups=order
    )
    turned_weight, own = pl.pallas_call(
        weights_kernel,
        out_shape=(
            jax.ShapeDtypeStruct((width_all, relations * width_all), jnp.bfloat16),
            jax.ShapeDtypeStruct((width_all, width), jnp.float32),
        ),
        in_specs=[VMEM, VMEM, VMEM, ANY],
        out_specs=(VMEM, VMEM),
        compiler_params=vmem_params(12),
        cost_estimate=pl.CostEstimate(flops=100_000_000, bytes_accessed=7 * MIB, transcendentals=0),
        name="weights",
    )(rel_weight, self_weight, features, token)
    partial_sum = pl.pallas_call(
        transform_kernel,
        out_shape=jax.ShapeDtypeStruct((width_all, width), jnp.float32),
        in_specs=[VMEM, VMEM, VMEM],
        out_specs=VMEM,
        compiler_params=vmem_params(8),
        name="transform",
    )(turned_weight, gathered, own)
    other = lax.ppermute(partial_sum, "rel", [(0, 1), (1, 0)])
    return jnp.maximum(partial_sum + other, 0.0).astype(jnp.bfloat16)


def solution(mesh):
    placed = (
        P(None, "feat"),
        P("rel", None, None),
        P("rel", None),
        P("rel", None),
        P("rel", None),
        P("rel", None, None, None),
        P("rel"),
        P("rel", "feat"),
    )
    return jax.shard_map(
        shards, mesh=mesh, in_specs=placed, out_specs=P(None, "feat"), check_vma=False
    )
```
